128 devices in a mesh: dp: 8 (over y, z_lo), fsdp: 16 (over z_hi, x, core).
Axes of the slice: x: 4, y: 4, z: 4 (z_hi: 2, z_lo: 2; z = z_hi * 2 + z_lo), core: 2. Of those that a mesh axis runs over, the one named last changes fastest.
Arguments:
- acts: bfloat16 [4096, 8192], P('dp', 'fsdp'), may hold values from -6 to 6
- grads_out: bfloat16 [4096, 12288], P('dp', 'fsdp'), may hold values from -0.0625 to 0.0625
- basis: bfloat16 [8192, 512], P('fsdp'), may hold values from -0.375 to 0.375
- first_moment: float32 [512, 12288], P('fsdp', 'dp'), may hold values from -6 to 6
- second_moment: float32 [512, 12288], P('fsdp', 'dp'), may hold values from 0.002 to 0.02
Outputs:
- update: bfloat16 [8192, 12288], P('fsdp', 'dp')
- moment_one: float32 [512, 12288], P('fsdp', 'dp')
- moment_two: float32 [512, 12288], P('fsdp', 'dp')
The draws below stay inside these ranges and needn't reach their ends.
All inputs are finite; a program needn't handle non-finite values.
Results may differ from the reference program's by a relative error of at most 0.0049.
Values may be sent and summed in bfloat16 or wider, within the bound.
A program may use at most 128 MiB of HBM per device.

```python
import math
import jax
import jax.numpy as jnp
from jax import lax

D = 8192
FFW = 12288
RANK = 512
TOKENS = 4096
N_DP = 8


def raised(drawn, key, source, target, blocks, factor):
    def block_of(dim):
        return (jnp.arange(drawn.shape[dim]) // (drawn.shape[dim] // blocks)).reshape((-1,) + (1,) * (drawn.ndim - 1 - dim))

    near = jax.random.permutation(key, blocks)[block_of(target)]
    far = (block_of(target) + blocks // 2) % blocks
    return jnp.where((block_of(source) == near) | (block_of(source) == far), factor * drawn, drawn)


def shard_levels(key, dims, split, low, high):
    gain, own = 1.0, jax.random.fold_in(key, 6)
    for position, shards_of in split:
        heights = jnp.exp(jax.random.uniform(jax.random.fold_in(own, position), (shards_of,), jnp.float32, low / len(split), high / len(split)))
        gain = gain * jnp.repeat(heights, dims[position] // shards_of).reshape([-1 if axis == position else 1 for axis in range(len(dims))])
    return gain


def gaussian(own_key, extent, scale, most, shards=(), dtype=jnp.bfloat16):
    result = jax.random.normal(own_key, extent, jnp.float32) * scale
    if len(shards) > 0:
        result = shard_levels(own_key, extent, shards, -0.22, 0.18) * result
    return jnp.clip(result, min=-most, max=most).astype(dtype)


def noise_with(own_key, dims, scale, bound, pieces, heavy, held_as=jnp.bfloat16):
    entries = scale * jax.random.normal(own_key, dims, jnp.float32)
    if pieces:
        entries = entries * shard_levels(own_key, dims, pieces, -0.22, 0.18)
    return jnp.clip(raised(entries, jax.random.fold_in(own_key, 3), *heavy), -bound, bound).astype(held_as)


def setup_inputs(seed: int = 0) -> dict:
    seeds = jax.random.split(jax.random.key(seed), 6)
    return {
        "acts": gaussian(seeds[0], (TOKENS, D), 1.0, 6.0, ((0, 8), (1, 16))),
        "grads_out": gaussian(seeds[1], (TOKENS, FFW), ((RANK / (D * TOKENS)) ** 0.5), 0.0625, ((0, 8), (1, 16))),
        "basis": noise_with(seeds[2], (D, RANK), RANK ** -0.5, 0.375, ((0, 16),), (0, 1, 16, 2.0)),
        "first_moment": gaussian(seeds[3], (RANK, FFW), 1.0, 6.0, ((0, 16), (1, 8)), jnp.float32),
        "second_moment": jnp.clip(jnp.exp(math.log(0.02) - 2.30258502 * jax.random.uniform(seeds[4], (RANK, FFW), jnp.float32) ** shard_levels(seeds[4], (RANK, FFW), ((0, 16), (1, 8)), -0.2, 0.2)), 0.002, 0.02),
    }


bias_one = 1.0 - 0.9 ** 10
bias_two = 1.0 - 0.999 ** 10
adam_eps = 1e-08
galore_scale = 0.25

def reference(acts, grads_out, basis, first_moment, second_moment):
    basis_wide = basis.astype(jnp.float32)
    width = FFW // N_DP
    blocks = []
    for index in range(N_DP):
        grad = jnp.dot(acts.T, grads_out[:, index * width:(index + 1) * width], preferred_element_type=jnp.float32)
        blocks.append(jnp.dot(basis_wide.T, grad, precision=lax.Precision.HIGHEST))
    projected = jnp.concatenate(blocks, axis=1)
    moment_one = 0.9 * first_moment + 0.1 * projected
    moment_two = 0.999 * second_moment + 0.001 * projected * projected
    normed = (moment_one / bias_one / (jnp.sqrt(moment_two / bias_two) + adam_eps)).astype(jnp.bfloat16)
    update = (galore_scale * jnp.dot(basis, normed, preferred_element_type=jnp.float32)).astype(jnp.bfloat16)
    return (update, moment_one, moment_two)
```

```python
import functools

import jax
import jax.numpy as jnp
from jax import lax
from jax.experimental import pallas as pl
from jax.experimental.pallas import tpu as pltpu
from jax.sharding import PartitionSpec as P

bias_one = 1.0 - 0.9**10
bias_two = 1.0 - 0.999**10
adam_eps = 1e-08
galore_scale = 0.25

MESH = pl.DeviceIdType.MESH
bf16, f32 = jnp.bfloat16, jnp.float32

CHIPS = 8
ROWS = 32
TOK = 512
WIDE = 1536
HALF = WIDE // 2
K = 4
W = WIDE // K


def kernel(
    acts_ref, g_ref, basis_ref, fm_ref, sm_ref,
    upd_ref, m1_ref, m2_ref,
    acts, basis, gfull, fm, sm, upd, m1, m2,
    pown, psend, precv, asend, arecv, pfull,
    q, qrecv, tsend, trecv, nfull,
    lsem, pair_s, pair_r, a_s, a_r, ag_s, ag_r, b_s, b_r, t_s, t_r, c_s, c_r, f_s, f_r,
):
    i, j = lax.axis_index("dp"), lax.axis_index("fsdp")
    m, c = j // 2, j % 2
    other = 1 - c
    pair = (i, 2 * m + other)

    def in_row(d):
        return lax.rem(m + d, CHIPS)

    def in_col(d):
        return lax.rem(i + d, CHIPS)

    def remote(src, dst, s, r, device):
        return pltpu.make_async_remote_copy(
            src_ref=src, dst_ref=dst, send_sem=s, recv_sem=r, device_id=device, device_id_type=MESH
        )

    loads = [
        pltpu.make_async_copy(acts_ref, acts, lsem.at[0]),
        pltpu.make_async_copy(basis_ref, basis, lsem.at[1]),
        pltpu.make_async_copy(g_ref, gfull.at[c], lsem.at[2]),
        pltpu.make_async_copy(fm_ref, fm, lsem.at[3]),
        pltpu.make_async_copy(sm_ref, sm, lsem.at[4]),
    ]
    for load in loads:
        load.start()

    barrier = pltpu.get_barrier_semaphore()
    pl.semaphore_signal(barrier, inc=1, device_id=pair, device_id_type=MESH)
    for d in range(1, CHIPS):
        pl.semaphore_signal(barrier, inc=1, device_id=(i, 2 * in_row(d) + c), device_id_type=MESH)
        pl.semaphore_signal(barrier, inc=1, device_id=(in_col(d), j), device_id_type=MESH)
    turned = (m, 2 * i + c)

    @pl.when(i != m)
    def _():
        pl.semaphore_signal(barrier, inc=1, device_id=turned, device_id_type=MESH)

    loads[0].wait()
    loads[1].wait()
    pown[...] = lax.dot_general(
        basis[...], acts[...], (((0,), (1,)), ((), ())), preferred_element_type=f32
    ).reshape(CHIPS, 2, ROWS, TOK)
    psend[...] = pown[:, pl.ds(other, 1)].reshape(CHIPS, ROWS, TOK).astype(bf16)

    @pl.when(i != m)
    def _():
        pl.semaphore_wait(barrier, 2 * CHIPS)

    @pl.when(i == m)
    def _():
        pl.semaphore_wait(barrier, 2 * CHIPS - 1)

    to_pair = remote(psend, precv, pair_s.at[0], pair_r.at[0], pair)
    to_pair.start()
    loads[2].wait()
    g_pair = remote(gfull.at[c], gfull.at[c], pair_s.at[1], pair_r.at[1], pair)
    g_pair.start()

    to_pair.wait()
    asend[...] = (pown[:, pl.ds(c, 1)].reshape(CHIPS, ROWS, TOK) + precv[...].astype(f32)).astype(bf16)
    a_copies = []
    for d in range(1, CHIPS):
        copy = remote(
            asend.at[in_row(d)], arecv.at[d], a_s.at[d], a_r.at[d], (i, 2 * in_row(d) + c)
        )
        copy.start()
        a_copies.append(copy)
    total = asend[m].astype(f32)
    for d in range(1, CHIPS):
        a_copies[d - 1].wait()
        total += arecv[d].astype(f32)
    pfull[m] = total.astype(bf16)
    ag_copies = []
    for d in range(1, CHIPS):
        copy = remote(
            pfull.at[m], pfull.at[m], ag_s.at[d], ag_r.at[d], (i, 2 * in_row(d) + c)
        )
        copy.start()
        ag_copies.append(copy)
    for d in range(1, CHIPS):
        ag_copies[d - 1].wait()
    g_pair.wait()

    b_copies = []
    for k in range(K):
        half, at = k * W // HALF, (k * W) % HALF
        q[k] = (
            jnp.dot(
                pfull[...].reshape(CHIPS * ROWS, TOK),
                gfull[half, :, at : at + W],
                preferred_element_type=f32,
            )
            .astype(bf16)
            .reshape(CHIPS, ROWS, W)
        )
        row = []
        for d in range(1, CHIPS):
            copy = remote(
                q.at[k, in_col(d)], qrecv.at[k, d], b_s.at[k, d], b_r.at[k, d], (in_col(d), j)
            )
            copy.start()
            row.append(copy)
        b_copies.append(row)
    loads[3].wait()
    loads[4].wait()

    def turn(k):
        return remote(tsend.at[k], trecv.at[k], t_s.at[k], t_r.at[k], turned)

    def reduce(k):
        total = q[k, i].astype(f32)
        for d in range(1, CHIPS):
            b_copies[k][d - 1].wait()
            total += qrecv[k, d].astype(f32)
        tsend[k] = total

        @pl.when(i != m)
        def _():
            turn(k).start()

        @pl.when(i == m)
        def _():
            trecv[k] = total

    c_copies = {}

    def moments(k):
        @pl.when(i != m)
        def _():
            turn(k).wait()

        cols = slice(k * W, (k + 1) * W)
        proj = trecv[k]
        one = 0.9 * fm[:, cols] + 0.1 * proj
        two = 0.999 * sm[:, cols] + 0.001 * proj * proj
        m1[:, cols] = one
        m2[:, cols] = two
        nfull[k, m, c] = (one / bias_one / (jnp.sqrt(two / bias_two) + adam_eps)).astype(bf16)
        mine = nfull.at[k, m, c]
        row = []
        for d in range(1, CHIPS):
            copy = remote(mine, mine, c_s.at[k, d], c_r.at[k, d], (i, 2 * in_row(d) + c))
            copy.start()
            row.append(copy)
        c_copies[k] = row

    f_copies = {}

    def share(k):
        for copy in c_copies[k]:
            copy.wait()
        mine = nfull.at[k, :, c]
        f_copies[k] = remote(mine, mine, f_s.at[k], f_r.at[k], pair)
        f_copies[k].start()

    stores = []

    def update(k):
        f_copies[k].wait()
        cols = slice(k * W, (k + 1) * W)
        upd[:, cols] = (
            galore_scale
            * jnp.dot(
                basis[...], nfull[k].reshape(CHIPS * 2 * ROWS, W), preferred_element_type=f32
            )
        ).astype(bf16)
        store = pltpu.make_async_copy(upd.at[:, cols], upd_ref.at[:, cols], lsem.at[5 + k])
        store.start()
        stores.append(store)

    for step in range(K + 3):
        if step < K:
            reduce(step)
        if 0 <= step - 1 < K:
            moments(step - 1)
            if step - 1 == K - 1:
                for n, (src, dst) in enumerate(((m1, m1_ref), (m2, m2_ref))):
                    store = pltpu.make_async_copy(src, dst, lsem.at[5 + K + n])
                    store.start()
                    stores.append(store)
        if 0 <= step - 2 < K:
            share(step - 2)
        if 0 <= step - 3 < K:
            update(step - 3)
    for store in stores:
        store.wait()


def shards(acts, grads_out, basis, first_moment, second_moment):
    any_space = pl.BlockSpec(memory_space=pl.ANY)
    dma = pltpu.SemaphoreType.DMA
    return pl.pallas_call(
        kernel,
        out_shape=(
            jax.ShapeDtypeStruct((TOK, WIDE), bf16),
            jax.ShapeDtypeStruct((ROWS, WIDE), f32),
            jax.ShapeDtypeStruct((ROWS, WIDE), f32),
        ),
        in_specs=[any_space] * 5,
        out_specs=(any_space,) * 3,
        scratch_shapes=[
            pltpu.VMEM((TOK, 512), bf16),
            pltpu.VMEM((512, 512), bf16),
            pltpu.VMEM((2, TOK, HALF), bf16),
            pltpu.VMEM((ROWS, WIDE), f32),
            pltpu.VMEM((ROWS, WIDE), f32),
            pltpu.VMEM((512, WIDE), bf16),
            pltpu.VMEM((ROWS, WIDE), f32),
            pltpu.VMEM((ROWS, WIDE), f32),
            pltpu.VMEM((CHIPS, 2, ROWS, TOK), f32),
            pltpu.VMEM((CHIPS, ROWS, TOK), bf16),
            pltpu.VMEM((CHIPS, ROWS, TOK), bf16),
            pltpu.VMEM((CHIPS, ROWS, TOK), bf16),
            pltpu.VMEM((CHIPS, ROWS, TOK), bf16),
            pltpu.VMEM((CHIPS, ROWS, TOK), bf16),
            pltpu.VMEM((K, CHIPS, ROWS, W), bf16),
            pltpu.VMEM((K, CHIPS, ROWS, W), bf16),
            pltpu.VMEM((K, ROWS, W), f32),
            pltpu.VMEM((K, ROWS, W), f32),
            pltpu.VMEM((K, CHIPS, 2, ROWS, W), bf16),
            dma((7 + K,)),
            dma((2,)),
            dma((2,)),
            dma((CHIPS,)),
            dma((CHIPS,)),
            dma((CHIPS,)),
            dma((CHIPS,)),
            dma((K, CHIPS)),
            dma((K, CHIPS)),
            dma((K,)),
            dma((K,)),
            dma((K, CHIPS)),
            dma((K, CHIPS)),
            dma((K,)),
            dma((K,)),
        ],
        compiler_params=pltpu.CompilerParams(
            collective_id=0, has_side_effects=True, vmem_limit_bytes=56 * 2**20
        ),
        cost_estimate=pl.CostEstimate(flops=2 * 10**9, bytes_accessed=4 * 2**20, transcendentals=0),
        name="galore_step",
    )(acts, grads_out, basis, first_moment, second_moment)


def solution(mesh):
    return jax.shard_map(
        shards,
        mesh=mesh,
        in_specs=(
            P("dp", "fsdp"),
            P("dp", "fsdp"),
            P("fsdp", None),
            P("fsdp", "dp"),
            P("fsdp", "dp"),
        ),
        out_specs=(P("fsdp", "dp"), P("fsdp", "dp"), P("fsdp", "dp")),
        check_vma=False,
    )
```

```python
import jax
import jax.numpy as jnp
from jax import lax
from jax.experimental import pallas as pl
from jax.experimental.pallas import tpu as pltpu
from jax.sharding import PartitionSpec as P

bias_one = 1.0 - 0.9**10
bias_two = 1.0 - 0.999**10
adam_eps = 1e-08
galore_scale = 0.25

MESH = pl.DeviceIdType.MESH
bf16, f32 = jnp.bfloat16, jnp.float32

CHIPS = 8
ROWS = 32
TOK = 512
DEEP = 512
WIDE = 1536
HALF = WIDE // 2
R = 2
RR = ROWS // R
K = 2
DIRECT = range(99)
W = WIDE // K
PARTS = [(r, k) for r in range(R) for k in range(K)]
LAGS = {"reduce": 0.0, "moments": 3.9, "forward": 6.6, "near": 6.9, "far": 9.3}
GAP = 8.4 / len(PARTS)
STEPS = sorted((lag + GAP * t, name, t) for name, lag in LAGS.items() for t in range(len(PARTS)))


def kernel(
    acts_ref, g_ref, basis_ref, fm_ref, sm_ref,
    upd_ref, m1_ref, m2_ref,
    acts, basis, g, fm, sm, upd, m1, m2,
    pown, psend, precv, asend, arecv, pfull,
    q, qrecv, tsend, trecv, nfull,
    lsem, p_s, p_r, g_s, g_r, a_s, a_r, ag_s, ag_r, b_s, b_r, t_s, t_r,
    c_s, c_r, z_s, z_r, d_s, d_r, f_s, f_r,
):
    i, j = lax.axis_index("dp"), lax.axis_index("fsdp")
    m, c = j // 2, lax.rem(j, 2)
    other = 1 - c
    y, z_lo, z_hi, x = i // 2, lax.rem(i, 2), m // 4, lax.rem(m, 4)
    pair = (i, 2 * m + other)

    rows = [lax.rem(m + d, CHIPS) for d in range(CHIPS)]
    cols_of = [lax.rem(i + d, CHIPS) for d in range(CHIPS)]
    along = [4 * z_hi + lax.rem(x + d, 4) for d in range(4)]
    over = lax.rem(m + 4, CHIPS)
    row_peers = [(i, 2 * to + c) for to in rows]
    col_peers = [(to, j) for to in cols_of]

    def block_of(at):
        x_to = lax.rem(x + 6 + at // 2 - 2 * z_hi - x // 2, 4)
        return 4 * lax.rem(z_hi + at + x, 2) + x_to

    blocks = [block_of(to) for to in cols_of]
    row_to = blocks[0]
    z_from, x_from = i // 4, lax.rem(i, 4)
    y_from = lax.rem(x + 6 - x_from + 2 * z_from + x_from // 2, 4)
    i_from = 2 * y_from + lax.rem(z_hi + z_from + x_from, 2)
    stays = jnp.logical_and(m == i, row_to == m)
    turned, comes = (m, 2 * row_to + c), (i_from, 2 * i + c)

    def remote(src, dst, s, r, device):
        return pltpu.make_async_remote_copy(
            src_ref=src, dst_ref=dst, send_sem=s, recv_sem=r, device_id=device, device_id_type=MESH
        )

    sent = []

    def got(copy):
        copy.wait_recv()
        sent.append(copy)

    g_here = g.at[:, pl.ds(pl.multiple_of(c * HALF, HALF), HALF)]
    loads = [
        pltpu.make_async_copy(acts_ref, acts, lsem.at[0]),
        pltpu.make_async_copy(basis_ref, basis, lsem.at[1]),
        pltpu.make_async_copy(g_ref, g_here, lsem.at[2]),
        pltpu.make_async_copy(fm_ref, fm, lsem.at[3]),
        pltpu.make_async_copy(sm_ref, sm, lsem.at[4]),
    ]
    for load in loads:
        load.start()

    barrier = pltpu.get_barrier_semaphore()
    pl.semaphore_signal(barrier, inc=1, device_id=pair, device_id_type=MESH)
    for d in range(1, CHIPS):
        pl.semaphore_signal(barrier, inc=1, device_id=row_peers[d], device_id_type=MESH)
        pl.semaphore_signal(barrier, inc=1, device_id=col_peers[d], device_id_type=MESH)

    @pl.when(jnp.logical_not(stays))
    def _():
        pl.semaphore_signal(barrier, inc=1, device_id=turned, device_id_type=MESH)
        pl.semaphore_signal(barrier, inc=1, device_id=comes, device_id_type=MESH)

    loads[0].wait()
    loads[1].wait()
    pown[...] = lax.dot_general(
        basis[...], acts[...], (((0,), (1,)), ((), ())), preferred_element_type=f32
    ).reshape(CHIPS, 2, ROWS, TOK)
    for r in range(R):
        psend[r] = pown[:, pl.ds(other, 1), r * RR : (r + 1) * RR].reshape(CHIPS, RR, TOK).astype(bf16)

    @pl.when(jnp.logical_not(stays))
    def _():
        pl.semaphore_wait(barrier, 2 * CHIPS + 1)

    @pl.when(stays)
    def _():
        pl.semaphore_wait(barrier, 2 * CHIPS - 1)

    to_pair = [remote(psend.at[r], precv.at[r], p_s.at[r], p_r.at[r], pair) for r in range(R)]
    for copy in to_pair:
        copy.start()
    loads[2].wait()
    g_pair = remote(g_here, g_here, g_s.at[0], g_r.at[0], pair)
    g_pair.start()

    a_copies = [
        [
            remote(
                asend.at[r, rows[d]],
                arecv.at[r, d],
                a_s.at[r, d],
                a_r.at[r, d],
                row_peers[d],
            )
            for d in range(1, CHIPS)
        ]
        for r in range(R)
    ]
    for r in range(R):
        got(to_pair[r])
        asend[r] = (
            pown[:, pl.ds(c, 1), r * RR : (r + 1) * RR].reshape(CHIPS, RR, TOK)
            + precv[r].astype(f32)
        ).astype(bf16)
        for copy in a_copies[r]:
            copy.start()
    ag_copies = [
        [
            remote(
                pfull.at[r, m],
                pfull.at[r, m],
                ag_s.at[r, d],
                ag_r.at[r, d],
                row_peers[d],
            )
            for d in range(1, CHIPS)
        ]
        for r in range(R)
    ]
    for r in range(R):
        total = asend[r, m].astype(f32)
        for d in range(1, CHIPS):
            got(a_copies[r][d - 1])
            total += arecv[r, d].astype(f32)
        pfull[r, m] = total.astype(bf16)
        for copy in ag_copies[r]:
            copy.start()

    b_copies = []
    for t, (r, k) in enumerate(PARTS):
        if k == 0:
            for copy in ag_copies[r]:
                got(copy)
        if t == 0:
            got(g_pair)
        q[t] = (
            jnp.dot(
                pfull[r].reshape(CHIPS * RR, TOK),
                g[:, k * W : (k + 1) * W],
                preferred_element_type=f32,
            )
            .astype(bf16)
            .reshape(CHIPS, RR, W)
        )
        b_copies.append(
            [
                remote(
                    q.at[t, blocks[d]],
                    qrecv.at[t, d],
                    b_s.at[t, d],
                    b_r.at[t, d],
                    col_peers[d],
                )
                for d in range(1, CHIPS)
            ]
        )
        for copy in b_copies[t]:
            copy.start()
    loads[3].wait()
    loads[4].wait()

    def turn(t):
        return remote(tsend.at[t], trecv.at[t], t_s.at[t], t_r.at[t], turned)

    def reduce(t):
        total = q[t, row_to].astype(f32)
        for d in range(1, CHIPS):
            got(b_copies[t][d - 1])
            total += qrecv[t, d].astype(f32)
        tsend[t] = total.astype(bf16)

        @pl.when(jnp.logical_not(stays))
        def _():
            turn(t).start()

        @pl.when(stays)
        def _():
            trecv[t] = total.astype(bf16)

    near_copies, far_copies, shares = {}, {}, {}
    lines = [slice(r * RR, (r + 1) * RR) for r in range(R)]

    def along_x(t, chip, s, r):
        block = nfull.at[PARTS[t][1], chip, c, lines[PARTS[t][0]]]
        copies = []
        for d in range(1, 4):
            copies.append(remote(block, block, s.at[t, d], r.at[t, d], (i, 2 * along[d] + c)))
            copies[-1].start()
        return copies

    def beyond(t):
        block = nfull.at[PARTS[t][1], m, c, lines[PARTS[t][0]]]
        copies = []
        for d in range(1, 4):
            to = lax.rem(along[d] + 4, CHIPS)
            copies.append(remote(block, block, d_s.at[t, d], d_r.at[t, d], (i, 2 * to + c)))
            copies[-1].start()
        return copies

    def across(t):
        mine = nfull.at[PARTS[t][1], m, c, lines[PARTS[t][0]]]
        return remote(mine, mine, z_s.at[t], z_r.at[t], (i, 2 * over + c))

    def to_other_core(t, first, n):
        part = nfull.at[PARTS[t][1], pl.ds(first, 4), c, lines[PARTS[t][0]]]
        shares[t, n] = remote(part, part, f_s.at[t, n], f_r.at[t, n], pair)
        shares[t, n].start()

    def moments(t):
        @pl.when(jnp.logical_not(stays))
        def _():
            turn(t).wait_recv()

        r, k = PARTS[t]
        cols = slice(k * W, (k + 1) * W)
        proj = trecv[t].astype(f32)
        one = 0.9 * fm[lines[r], cols] + 0.1 * proj
        two = 0.999 * sm[lines[r], cols] + 0.001 * proj * proj
        nfull[k, m, c, lines[r]] = (
            one / bias_one / (jnp.sqrt(two / bias_two) + adam_eps)
        ).astype(bf16)
        across(t).start()
        near_copies[t] = along_x(t, m, c_s, c_r)
        if t in DIRECT:
            far_copies[t] = beyond(t)
        m1[lines[r], cols] = one
        m2[lines[r], cols] = two

    def forward(t):
        if t not in DIRECT:
            got(across(t))
            far_copies[t] = along_x(t, over, d_s, d_r)

    def near(t):
        for copy in near_copies[t]:
            got(copy)
        to_other_core(t, 4 * z_hi, 0)

    stores = []

    def store(src, dst):
        stores.append(pltpu.make_async_copy(src, dst, lsem.at[5 + len(stores)]))
        stores[-1].start()

    def far(t):
        if t in DIRECT:
            got(across(t))
        for copy in far_copies[t]:
            got(copy)
        to_other_core(t, 4 * (1 - z_hi), 1)

    def update(k):
        for t in range(len(PARTS)):
            if PARTS[t][1] == k:
                got(shares[t, 0])
                got(shares[t, 1])
        cols = slice(k * W, (k + 1) * W)
        upd[:, cols] = (
            galore_scale
            * jnp.dot(
                basis[...], nfull[k].reshape(CHIPS * 2 * ROWS, W), preferred_element_type=f32
            )
        ).astype(bf16)
        store(upd.at[:, cols], upd_ref.at[:, cols])

    steps = {"reduce": reduce, "moments": moments, "forward": forward, "near": near, "far": far}
    pending = []
    for _, name, t in STEPS:
        steps[name](t)
        if (name, t) == ("moments", len(PARTS) - 1):
            store(m1, m1_ref)
            store(m2, m2_ref)
        if pending and name in ("near", "far"):
            update(pending.pop())
        if name == "far" and PARTS[t][0] == R - 1:
            pending.append(PARTS[t][1])
    for k in pending:
        update(k)
    for copy in stores:
        copy.wait()
    for copy in sent:
        copy.wait_send()

    @pl.when(jnp.logical_not(stays))
    def _():
        for t in range(len(PARTS)):
            turn(t).wait_send()


def shards(acts, grads_out, basis, first_moment, second_moment):
    def vmem(shape, dtype):
        return pltpu.VMEM(shape, dtype)

    def dma(*shape):
        return pltpu.SemaphoreType.DMA(shape)

    n = len(PARTS)
    return pl.pallas_call(
        kernel,
        out_shape=(
            jax.ShapeDtypeStruct((DEEP, WIDE), bf16),
            jax.ShapeDtypeStruct((ROWS, WIDE), f32),
            jax.ShapeDtypeStruct((ROWS, WIDE), f32),
        ),
        in_specs=[pl.BlockSpec(memory_space=IN_SPACE)] * 5,
        out_specs=(pl.BlockSpec(memory_space=pl.ANY),) * 3,
        scratch_shapes=[
            vmem((TOK, DEEP), bf16),
            vmem((DEEP, 512), bf16),
            vmem((TOK, WIDE), bf16),
            vmem((ROWS, WIDE), f32),
            vmem((ROWS, WIDE), f32),
            vmem((DEEP, WIDE), bf16),
            vmem((ROWS, WIDE), f32),
            vmem((ROWS, WIDE), f32),
            vmem((CHIPS, 2, ROWS, TOK), f32),
            vmem((R, CHIPS, RR, TOK), bf16),
            vmem((R, CHIPS, RR, TOK), bf16),
            vmem((R, CHIPS, RR, TOK), bf16),
            vmem((R, CHIPS, RR, TOK), bf16),
            vmem((R, CHIPS, RR, TOK), bf16),
            vmem((n, CHIPS, RR, W), bf16),
            vmem((n, CHIPS, RR, W), bf16),
            vmem((n, RR, W), bf16),
            vmem((n, RR, W), bf16),
            vmem((K, CHIPS, 2, ROWS, W), bf16),
            dma(7 + K),
            dma(R),
            dma(R),
            dma(1),
            dma(1),
            dma(R, CHIPS),
            dma(R, CHIPS),
            dma(R, CHIPS),
            dma(R, CHIPS),
            dma(n, CHIPS),
            dma(n, CHIPS),
            dma(n),
            dma(n),
            dma(n, 4),
            dma(n, 4),
            dma(n),
            dma(n),
            dma(n, 4),
            dma(n, 4),
            dma(n, 2),
            dma(n, 2),
        ],
        compiler_params=pltpu.CompilerParams(
            collective_id=0, has_side_effects=True, vmem_limit_bytes=LIMIT * 2**20
        ),
        cost_estimate=pl.CostEstimate(flops=2 * 10**9, bytes_accessed=4 * 2**20, transcendentals=0),
        name="galore_step",
    )(*(pltpu.with_memory_space_constraint(v, pltpu.HBM) for v in (acts, grads_out, basis, first_moment, second_moment)))


IN_SPACE = pl.ANY
LIMIT = 24


def solution(mesh):
    return jax.shard_map(
        shards,
        mesh=mesh,
        in_specs=(
            P("dp", "fsdp"),
            P("dp", "fsdp"),
            P("fsdp", None),
            P("fsdp", "dp"),
            P("fsdp", "dp"),
        ),
        out_specs=(P("fsdp", "dp"), P("fsdp", "dp"), P("fsdp", "dp")),
        check_vma=False,
    )
```

```python
import jax
import jax.numpy as jnp
from jax import lax
from jax.experimental import pallas as pl
from jax.experimental.pallas import tpu as pltpu
from jax.sharding import PartitionSpec as P

bias_one = 1.0 - 0.9**10
bias_two = 1.0 - 0.999**10
adam_eps = 1e-08
galore_scale = 0.25

MESH = pl.DeviceIdType.MESH
bf16, f32 = jnp.bfloat16, jnp.float32

CHIPS = 8
ROWS = 32
TOK = 512
DEEP = 512
WIDE = 1536
HALF = WIDE // 2
R = 2
RR = ROWS // R
K = 2
W = WIDE // K
PARTS = [(r, k) for r in range(R) for k in range(K)]
LAGS = {"reduce": 0.0, "moments": 3.9, "near": 6.9, "far": 9.3}
FLUSH = {("reduce", 3), ("moments", 3), ("far", 3)}
FAR_FIRST = [(0, 0), (1, 2), (1, 1), (1, 3), (0, 2), (1, 0), (0, 1), (0, 3)]
GAP = 8.4 / len(PARTS)
STEPS = sorted((lag + GAP * t, name, t) for name, lag in LAGS.items() for t in range(len(PARTS)))


def new_moments(first, second, proj):
    return 0.9 * first + 0.1 * proj, 0.999 * second + 0.001 * proj * proj


def kernel(
    acts_ref, g_ref, basis_ref, fm_ref, sm_ref,
    upd, proj_ref,
    acts, basis, g, fm, sm,
    pown, psend, precv, asend, arecv, pfull,
    q, qrecv, tsend, trecv, nfull,
    lsem, p_s, p_r, g_s, g_r, a_s, a_r, ag_s, ag_r, b_s, b_r, t_s, t_r,
    c_s, c_r, z_s, z_r, d_s, d_r, f_s, f_r,
):
    i, j = lax.axis_index("dp"), lax.axis_index("fsdp")
    m, c = j // 2, lax.rem(j, 2)
    other = 1 - c
    y, z_lo, z_hi, x = i // 2, lax.rem(i, 2), m // 4, lax.rem(m, 4)
    pair = (i, 2 * m + other)

    rows = [4 * lax.rem(z_hi + dz, 2) + lax.rem(x + dx, 4) for dz, dx in FAR_FIRST]
    cols_of = [2 * lax.rem(y + dy, 4) + lax.rem(z_lo + dz, 2) for dz, dy in FAR_FIRST]
    along = [4 * z_hi + lax.rem(x + d, 4) for d in range(4)]
    over = lax.rem(m + 4, CHIPS)
    row_peers = [(i, 2 * to + c) for to in rows]
    col_peers = [(to, j) for to in cols_of]

    def block_of(at):
        x_to = lax.rem(x + 6 + at // 2 - 2 * z_hi - x // 2, 4)
        return 4 * lax.rem(z_hi + at + x, 2) + x_to

    blocks = [block_of(to) for to in cols_of]
    row_to = blocks[0]
    z_from, x_from = i // 4, lax.rem(i, 4)
    y_from = lax.rem(x + 6 - x_from + 2 * z_from + x_from // 2, 4)
    i_from = 2 * y_from + lax.rem(z_hi + z_from + x_from, 2)
    stays = jnp.logical_and(m == i, row_to == m)
    turned, comes = (m, 2 * row_to + c), (i_from, 2 * i + c)

    def remote(src, dst, s, r, device):
        return pltpu.make_async_remote_copy(
            src_ref=src, dst_ref=dst, send_sem=s, recv_sem=r, device_id=device, device_id_type=MESH
        )

    sent = []

    def got(copy):
        copy.wait_recv()
        sent.append(copy)

    def flush():
        while sent:
            sent.pop(0).wait_send()

    g_here = g.at[:, pl.ds(pl.multiple_of(c * HALF, HALF), HALF)]
    loads = [
        pltpu.make_async_copy(acts_ref, acts, lsem.at[0]),
        pltpu.make_async_copy(basis_ref, basis, lsem.at[1]),
        pltpu.make_async_copy(g_ref, g_here, lsem.at[2]),
        pltpu.make_async_copy(fm_ref, fm, lsem.at[3]),
        pltpu.make_async_copy(sm_ref, sm, lsem.at[4]),
    ]
    for load in loads:
        load.start()

    barrier = pltpu.get_barrier_semaphore()
    for d in range(1, CHIPS):
        pl.semaphore_signal(barrier, inc=1, device_id=row_peers[d], device_id_type=MESH)
        pl.semaphore_signal(barrier, inc=1, device_id=col_peers[d], device_id_type=MESH)

    @pl.when(jnp.logical_not(stays))
    def _():
        pl.semaphore_signal(barrier, inc=1, device_id=turned, device_id_type=MESH)
        pl.semaphore_signal(barrier, inc=1, device_id=comes, device_id_type=MESH)

    pl.semaphore_signal(barrier, inc=1, device_id=pair, device_id_type=MESH)

    loads[0].wait()
    loads[1].wait()
    pown[...] = lax.dot_general(
        basis[...], acts[...], (((0,), (1,)), ((), ())), preferred_element_type=f32
    ).reshape(CHIPS, 2, ROWS, TOK)
    for r in range(R):
        psend[r] = pown[:, pl.ds(other, 1), r * RR : (r + 1) * RR].reshape(CHIPS, RR, TOK).astype(bf16)

    @pl.when(jnp.logical_not(stays))
    def _():
        pl.semaphore_wait(barrier, 2 * CHIPS + 1)

    @pl.when(stays)
    def _():
        pl.semaphore_wait(barrier, 2 * CHIPS - 1)

    to_pair = [remote(psend.at[r], precv.at[r], p_s.at[r], p_r.at[r], pair) for r in range(R)]
    for copy in to_pair:
        copy.start()
    loads[2].wait()
    g_pair = remote(g_here, g_here, g_s.at[0], g_r.at[0], pair)
    g_pair.start()

    a_copies = [
        [
            remote(
                asend.at[r, rows[d]],
                arecv.at[r, d],
                a_s.at[r, d],
                a_r.at[r, d],
                row_peers[d],
            )
            for d in range(1, CHIPS)
        ]
        for r in range(R)
    ]
    for r in range(R):
        got(to_pair[r])
        asend[r] = (
            pown[:, pl.ds(c, 1), r * RR : (r + 1) * RR].reshape(CHIPS, RR, TOK)
            + precv[r].astype(f32)
        ).astype(bf16)
        for copy in a_copies[r]:
            copy.start()
    ag_copies = [
        [
            remote(
                pfull.at[r, m],
                pfull.at[r, m],
                ag_s.at[r, d],
                ag_r.at[r, d],
                row_peers[d],
            )
            for d in range(1, CHIPS)
        ]
        for r in range(R)
    ]
    for r in range(R):
        total = asend[r, m].astype(f32)
        for d in range(1, CHIPS):
            got(a_copies[r][d - 1])
            total += arecv[r, d].astype(f32)
        pfull[r, m] = total.astype(bf16)
        for copy in ag_copies[r]:
            copy.start()

    b_copies = []
    for t, (r, k) in enumerate(PARTS):
        if k == 0:
            for copy in ag_copies[r]:
                got(copy)
        if t == 0:
            got(g_pair)
        q[t] = (
            jnp.dot(
                pfull[r].reshape(CHIPS * RR, TOK),
                g[:, k * W : (k + 1) * W],
                preferred_element_type=f32,
            )
            .astype(bf16)
            .reshape(CHIPS, RR, W)
        )
        b_copies.append(
            [
                remote(
                    q.at[t, blocks[d]],
                    qrecv.at[t, d],
                    b_s.at[t, d],
                    b_r.at[t, d],
                    col_peers[d],
                )
                for d in range(1, CHIPS)
            ]
        )
        for copy in b_copies[t]:
            copy.start()
    loads[3].wait()
    loads[4].wait()
    flush()

    def turn(t):
        return remote(tsend.at[t], trecv.at[t], t_s.at[t], t_r.at[t], turned)

    def reduce(t):
        total = q[t, row_to].astype(f32)
        for d in range(1, CHIPS):
            got(b_copies[t][d - 1])
            total += qrecv[t, d].astype(f32)
        tsend[t] = total.astype(bf16)

        @pl.when(jnp.logical_not(stays))
        def _():
            turn(t).start()

        @pl.when(stays)
        def _():
            trecv[t] = total.astype(bf16)

    near_copies, far_copies, shares = {}, {}, {}
    lines = [slice(r * RR, (r + 1) * RR) for r in range(R)]

    def along_x(t):
        block = nfull.at[PARTS[t][1], m, c, lines[PARTS[t][0]]]
        copies = []
        for d in (2, 1, 3):
            copies.append(remote(block, block, c_s.at[t, d], c_r.at[t, d], (i, 2 * along[d] + c)))
            copies[-1].start()
        return copies

    def beyond(t):
        block = nfull.at[PARTS[t][1], m, c, lines[PARTS[t][0]]]
        copies = []
        for d in (2, 1, 3):
            to = lax.rem(along[d] + 4, CHIPS)
            copies.append(remote(block, block, d_s.at[t, d], d_r.at[t, d], (i, 2 * to + c)))
            copies[-1].start()
        return copies

    def across(t):
        mine = nfull.at[PARTS[t][1], m, c, lines[PARTS[t][0]]]
        return remote(mine, mine, z_s.at[t], z_r.at[t], (i, 2 * over + c))

    def to_other_core(t, first, n):
        part = nfull.at[PARTS[t][1], pl.ds(first, 4), c, lines[PARTS[t][0]]]
        shares[t, n] = remote(part, part, f_s.at[t, n], f_r.at[t, n], pair)
        shares[t, n].start()

    def moments(t):
        @pl.when(jnp.logical_not(stays))
        def _():
            turn(t).wait_recv()

        r, k = PARTS[t]
        cols = slice(k * W, (k + 1) * W)
        proj = trecv[t].astype(f32)
        one, two = new_moments(fm[lines[r], cols], sm[lines[r], cols], proj)
        nfull[k, m, c, lines[r]] = (
            one / bias_one / (jnp.sqrt(two / bias_two) + adam_eps)
        ).astype(bf16)
        far_copies[t] = beyond(t)
        across(t).start()
        near_copies[t] = along_x(t)
        proj_ref[lines[r], cols] = proj

    def near(t):
        for copy in near_copies[t]:
            got(copy)
        to_other_core(t, 4 * z_hi, 0)

    def far(t):
        got(across(t))
        for copy in far_copies[t]:
            got(copy)
        to_other_core(t, 4 * (1 - z_hi), 1)

    def update(k):
        for t in range(len(PARTS)):
            if PARTS[t][1] == k:
                got(shares[t, 0])
                got(shares[t, 1])
        cols = slice(k * W, (k + 1) * W)
        upd[:, cols] = (
            galore_scale
            * jnp.dot(
                basis[...], nfull[k].reshape(CHIPS * 2 * ROWS, W), preferred_element_type=f32
            )
        ).astype(bf16)

    steps = {"reduce": reduce, "moments": moments, "near": near, "far": far}
    pending = []
    for _, name, t in STEPS:
        steps[name](t)
        if (name, t) in FLUSH:
            flush()
        if pending and name in ("near", "far"):
            update(pending.pop())
        if name == "far" and PARTS[t][0] == R - 1:
            pending.append(PARTS[t][1])
    for k in pending:
        update(k)
    flush()

    @pl.when(jnp.logical_not(stays))
    def _():
        for t in range(len(PARTS)):
            turn(t).wait_send()


def shards(acts, grads_out, basis, first_moment, second_moment):
    def vmem(shape, dtype):
        return pltpu.VMEM(shape, dtype)

    def dma(*shape):
        return pltpu.SemaphoreType.DMA(shape)

    n = len(PARTS)
    update, proj = pl.pallas_call(
        kernel,
        out_shape=(
            jax.ShapeDtypeStruct((DEEP, WIDE), bf16),
            jax.ShapeDtypeStruct((ROWS, WIDE), f32),
        ),
        in_specs=[pl.BlockSpec(memory_space=IN_SPACE)] * 5,
        out_specs=(pl.BlockSpec(memory_space=pltpu.VMEM),) * 2,
        scratch_shapes=[
            vmem((TOK, DEEP), bf16),
            vmem((DEEP, 512), bf16),
            vmem((TOK, WIDE), bf16),
            vmem((ROWS, WIDE), f32),
            vmem((ROWS, WIDE), f32),
            vmem((CHIPS, 2, ROWS, TOK), f32),
            vmem((R, CHIPS, RR, TOK), bf16),
            vmem((R, CHIPS, RR, TOK), bf16),
            vmem((R, CHIPS, RR, TOK), bf16),
            vmem((R, CHIPS, RR, TOK), bf16),
            vmem((R, CHIPS, RR, TOK), bf16),
            vmem((n, CHIPS, RR, W), bf16),
            vmem((n, CHIPS, RR, W), bf16),
            vmem((n, RR, W), bf16),
            vmem((n, RR, W), bf16),
            vmem((K, CHIPS, 2, ROWS, W), bf16),
            dma(5),
            dma(R),
            dma(R),
            dma(1),
            dma(1),
            dma(R, CHIPS),
            dma(R, CHIPS),
            dma(R, CHIPS),
            dma(R, CHIPS),
            dma(n, CHIPS),
            dma(n, CHIPS),
            dma(n),
            dma(n),
            dma(n, 4),
            dma(n, 4),
            dma(n),
            dma(n),
            dma(n, 4),
            dma(n, 4),
            dma(n, 2),
            dma(n, 2),
        ],
        compiler_params=pltpu.CompilerParams(
            collective_id=0, has_side_effects=True, vmem_limit_bytes=LIMIT * 2**20
        ),
        cost_estimate=pl.CostEstimate(flops=2 * 10**9, bytes_accessed=4 * 2**20, transcendentals=0),
        name="galore_step",
    )(*(pltpu.with_memory_space_constraint(v, pltpu.HBM) for v in (acts, grads_out, basis, first_moment, second_moment)))
    return update, *new_moments(first_moment, second_moment, proj)


IN_SPACE = pl.ANY
LIMIT = 24


def solution(mesh):
    return jax.shard_map(
        shards,
        mesh=mesh,
        in_specs=(
            P("dp", "fsdp"),
            P("dp", "fsdp"),
            P("fsdp", None),
            P("fsdp", "dp"),
            P("fsdp", "dp"),
        ),
        out_specs=(P("fsdp", "dp"), P("fsdp", "dp"), P("fsdp", "dp")),
        check_vma=False,
    )
```

```python
import jax
import jax.numpy as jnp
from jax import lax
from jax.experimental import pallas as pl
from jax.experimental.pallas import tpu as pltpu
from jax.sharding import PartitionSpec as P

bias_one = 1.0 - 0.9**10
bias_two = 1.0 - 0.999**10
adam_eps = 1e-08
galore_scale = 0.25

MESH = pl.DeviceIdType.MESH
bf16, f32 = jnp.bfloat16, jnp.float32

CHIPS = 8
ROWS = 32
TOK = 512
DEEP = 512
WIDE = 1536
HALF = WIDE // 2
R = 2
RR = ROWS // R
K = 2
W = WIDE // K
PARTS = [(r, k) for r in range(R) for k in range(K)]
LAGS = {"reduce": 0.0, "moments": 3.9, "near": 6.9, "far": 9.3}
FLUSH = {("reduce", 3), ("moments", 3), ("far", 3)}
FAR_FIRST = [(0, 0), (1, 2), (1, 1), (1, 3), (0, 2), (1, 0), (0, 1), (0, 3)]
GAP = 8.4 / len(PARTS)
STEPS = sorted((lag + GAP * t, name, t) for name, lag in LAGS.items() for t in range(len(PARTS)))


def new_moments(first, second, proj):
    return 0.9 * first + 0.1 * proj, 0.999 * second + 0.001 * proj * proj


def kernel(
    acts_ref, g_ref, basis_ref, fm_ref, sm_ref,
    upd, proj_ref,
    acts, basis, g, fm, sm,
    pown, psend, precv, asend, arecv, pfull,
    q, qrecv, tsend, trecv, nfull,
    lsem, p_s, p_r, g_s, g_r, a_s, a_r, ag_s, ag_r, b_s, b_r, t_s, t_r,
    c_s, c_r, d_s, d_r, f_s, f_r,
):
    i, j = lax.axis_index("dp"), lax.axis_index("fsdp")
    m, c = j // 2, lax.rem(j, 2)
    other = 1 - c
    y, z_lo, z_hi, x = i // 2, lax.rem(i, 2), m // 4, lax.rem(m, 4)
    pair = (i, 2 * m + other)

    rows = [4 * lax.rem(z_hi + dz, 2) + lax.rem(x + dx, 4) for dz, dx in FAR_FIRST]
    cols_of = [2 * lax.rem(y + dy, 4) + lax.rem(z_lo + dz, 2) for dz, dy in FAR_FIRST]
    along = [4 * z_hi + lax.rem(x + d, 4) for d in range(4)]
    over = lax.rem(m + 4, CHIPS)
    row_peers = [(i, 2 * to + c) for to in rows]
    col_peers = [(to, j) for to in cols_of]

    def block_of(at):
        x_to = lax.rem(x + 6 + at // 2 - 2 * z_hi - x // 2, 4)
        return 4 * lax.rem(z_hi + at + x, 2) + x_to

    blocks = [block_of(to) for to in cols_of]
    row_to = blocks[0]
    z_from, x_from = i // 4, lax.rem(i, 4)
    y_from = lax.rem(x + 6 - x_from + 2 * z_from + x_from // 2, 4)
    i_from = 2 * y_from + lax.rem(z_hi + z_from + x_from, 2)
    stays = jnp.logical_and(m == i, row_to == m)
    turned, comes = (m, 2 * row_to + c), (i_from, 2 * i + c)

    def remote(src, dst, s, r, device):
        return pltpu.make_async_remote_copy(
            src_ref=src, dst_ref=dst, send_sem=s, recv_sem=r, device_id=device, device_id_type=MESH
        )

    sent = []

    def got(copy):
        copy.wait_recv()
        sent.append(copy)

    def got_all(ref, s, r):
        got(remote(ref, ref, s, r, pair))

    def flush():
        while sent:
            sent.pop(0).wait_send()

    g_here = g.at[:, pl.ds(pl.multiple_of(c * HALF, HALF), HALF)]
    loads = [
        pltpu.make_async_copy(acts_ref, acts, lsem.at[0]),
        pltpu.make_async_copy(basis_ref, basis, lsem.at[1]),
        pltpu.make_async_copy(g_ref, g_here, lsem.at[2]),
        pltpu.make_async_copy(fm_ref, fm, lsem.at[3]),
        pltpu.make_async_copy(sm_ref, sm, lsem.at[4]),
    ]
    for load in loads:
        load.start()

    barrier = pltpu.get_barrier_semaphore()
    for d in range(1, CHIPS):
        pl.semaphore_signal(barrier, inc=1, device_id=row_peers[d], device_id_type=MESH)
        pl.semaphore_signal(barrier, inc=1, device_id=col_peers[d], device_id_type=MESH)

    @pl.when(jnp.logical_not(stays))
    def _():
        pl.semaphore_signal(barrier, inc=1, device_id=turned, device_id_type=MESH)
        pl.semaphore_signal(barrier, inc=1, device_id=comes, device_id_type=MESH)

    pl.semaphore_signal(barrier, inc=1, device_id=pair, device_id_type=MESH)

    loads[0].wait()
    loads[1].wait()
    pown[...] = lax.dot_general(
        basis[...], acts[...], (((0,), (1,)), ((), ())), preferred_element_type=f32
    ).reshape(CHIPS, 2, ROWS, TOK)
    for r in range(R):
        psend[r] = pown[:, pl.ds(other, 1), r * RR : (r + 1) * RR].reshape(CHIPS, RR, TOK).astype(bf16)

    @pl.when(jnp.logical_not(stays))
    def _():
        pl.semaphore_wait(barrier, 2 * CHIPS + 1)

    @pl.when(stays)
    def _():
        pl.semaphore_wait(barrier, 2 * CHIPS - 1)

    to_pair = [remote(psend.at[r], precv.at[r], p_s.at[r], p_r.at[r], pair) for r in range(R)]
    for copy in to_pair:
        copy.start()
    loads[2].wait()
    g_pair = remote(g_here, g_here, g_s.at[0], g_r.at[0], pair)
    g_pair.start()

    a_copies = [
        [
            remote(
                asend.at[r, rows[d]],
                arecv.at[r, d],
                a_s.at[r],
                a_r.at[r],
                row_peers[d],
            )
            for d in range(1, CHIPS)
        ]
        for r in range(R)
    ]
    for r in range(R):
        got(to_pair[r])
        asend[r] = (
            pown[:, pl.ds(c, 1), r * RR : (r + 1) * RR].reshape(CHIPS, RR, TOK)
            + precv[r].astype(f32)
        ).astype(bf16)
        for copy in a_copies[r]:
            copy.start()
    ag_copies = [
        [
            remote(
                pfull.at[r, m],
                pfull.at[r, m],
                ag_s.at[r],
                ag_r.at[r],
                row_peers[d],
            )
            for d in range(1, CHIPS)
        ]
        for r in range(R)
    ]
    for r in range(R):
        total = asend[r, m].astype(f32)
        got_all(arecv.at[r, pl.ds(1, CHIPS - 1)], a_s.at[r], a_r.at[r])
        for d in range(1, CHIPS):
            total += arecv[r, d].astype(f32)
        pfull[r, m] = total.astype(bf16)
        for copy in ag_copies[r]:
            copy.start()

    b_copies = []
    for t, (r, k) in enumerate(PARTS):
        if k == 0:
            got_all(arecv.at[r, pl.ds(1, CHIPS - 1)], ag_s.at[r], ag_r.at[r])
        if t == 0:
            got(g_pair)
        q[t] = (
            jnp.dot(
                pfull[r].reshape(CHIPS * RR, TOK),
                g[:, k * W : (k + 1) * W],
                preferred_element_type=f32,
            )
            .astype(bf16)
            .reshape(CHIPS, RR, W)
        )
        b_copies.append(
            [
                remote(
                    q.at[t, blocks[d]],
                    qrecv.at[t, d],
                    b_s.at[t],
                    b_r.at[t],
                    col_peers[d],
                )
                for d in range(1, CHIPS)
            ]
        )
        for copy in b_copies[t]:
            copy.start()
    loads[3].wait()
    loads[4].wait()
    flush()

    def turn(t):
        return remote(tsend.at[t], trecv.at[t], t_s.at[t], t_r.at[t], turned)

    def reduce(t):
        total = q[t, row_to].astype(f32)
        got_all(qrecv.at[t, pl.ds(1, CHIPS - 1)], b_s.at[t], b_r.at[t])
        for d in range(1, CHIPS):
            total += qrecv[t, d].astype(f32)
        tsend[t] = total.astype(bf16)

        @pl.when(jnp.logical_not(stays))
        def _():
            turn(t).start()

        @pl.when(stays)
        def _():
            trecv[t] = total.astype(bf16)

    near_copies, far_copies, shares = {}, {}, {}
    lines = [slice(r * RR, (r + 1) * RR) for r in range(R)]

    def along_x(t):
        block = nfull.at[PARTS[t][1], m, c, lines[PARTS[t][0]]]
        copies = []
        for d in (2, 1, 3):
            copies.append(remote(block, block, c_s.at[t], c_r.at[t], (i, 2 * along[d] + c)))
            copies[-1].start()
        return copies

    def beyond(t):
        block = nfull.at[PARTS[t][1], m, c, lines[PARTS[t][0]]]
        copies = []
        for d in (2, 1, 3):
            to = lax.rem(along[d] + 4, CHIPS)
            copies.append(remote(block, block, d_s.at[t], d_r.at[t], (i, 2 * to + c)))
            copies[-1].start()
        return copies

    def across(t):
        mine = nfull.at[PARTS[t][1], m, c, lines[PARTS[t][0]]]
        return remote(mine, mine, d_s.at[t], d_r.at[t], (i, 2 * over + c))

    def to_other_core(t, first, n):
        part = nfull.at[PARTS[t][1], pl.ds(first, 4), c, lines[PARTS[t][0]]]
        shares[t, n] = remote(part, part, f_s.at[t, n], f_r.at[t, n], pair)
        shares[t, n].start()

    def moments(t):
        @pl.when(jnp.logical_not(stays))
        def _():
            turn(t).wait_recv()

        r, k = PARTS[t]
        cols = slice(k * W, (k + 1) * W)
        proj = trecv[t].astype(f32)
        one, two = new_moments(fm[lines[r], cols], sm[lines[r], cols], proj)
        nfull[k, m, c, lines[r]] = (
            one / bias_one / (jnp.sqrt(two / bias_two) + adam_eps)
        ).astype(bf16)
        far_copies[t] = beyond(t)
        across(t).start()
        near_copies[t] = along_x(t)
        proj_ref[lines[r], cols] = proj

    def near(t):
        got_all(nfull.at[PARTS[t][1], pl.ds(0, 3), c, lines[PARTS[t][0]]], c_s.at[t], c_r.at[t])
        to_other_core(t, 4 * z_hi, 0)

    def far(t):
        got_all(nfull.at[PARTS[t][1], pl.ds(0, 4), c, lines[PARTS[t][0]]], d_s.at[t], d_r.at[t])
        to_other_core(t, 4 * (1 - z_hi), 1)

    def update(k):
        for t in range(len(PARTS)):
            if PARTS[t][1] == k:
                got(shares[t, 0])
                got(shares[t, 1])
        cols = slice(k * W, (k + 1) * W)
        upd[:, cols] = (
            galore_scale
            * jnp.dot(
                basis[...], nfull[k].reshape(CHIPS * 2 * ROWS, W), preferred_element_type=f32
            )
        ).astype(bf16)

    steps = {"reduce": reduce, "moments": moments, "near": near, "far": far}
    pending = []
    for _, name, t in STEPS:
        steps[name](t)
        if (name, t) in FLUSH:
            flush()
        if pending and name in ("near", "far"):
            update(pending.pop())
        if name == "far" and PARTS[t][0] == R - 1:
            pending.append(PARTS[t][1])
    for k in pending:
        update(k)
    flush()

    @pl.when(jnp.logical_not(stays))
    def _():
        for t in range(len(PARTS)):
            turn(t).wait_send()


def shards(acts, grads_out, basis, first_moment, second_moment):
    def vmem(shape, dtype):
        return pltpu.VMEM(shape, dtype)

    def dma(*shape):
        return pltpu.SemaphoreType.DMA(shape)

    n = len(PARTS)
    update, proj = pl.pallas_call(
        kernel,
        out_shape=(
            jax.ShapeDtypeStruct((DEEP, WIDE), bf16),
            jax.ShapeDtypeStruct((ROWS, WIDE), f32),
        ),
        in_specs=[pl.BlockSpec(memory_space=IN_SPACE)] * 5,
        out_specs=(pl.BlockSpec(memory_space=pltpu.VMEM),) * 2,
        scratch_shapes=[
            vmem((TOK, DEEP), bf16),
            vmem((DEEP, 512), bf16),
            vmem((TOK, WIDE), bf16),
            vmem((ROWS, WIDE), f32),
            vmem((ROWS, WIDE), f32),
            vmem((CHIPS, 2, ROWS, TOK), f32),
            vmem((R, CHIPS, RR, TOK), bf16),
            vmem((R, CHIPS, RR, TOK), bf16),
            vmem((R, CHIPS, RR, TOK), bf16),
            vmem((R, CHIPS, RR, TOK), bf16),
            vmem((R, CHIPS, RR, TOK), bf16),
            vmem((n, CHIPS, RR, W), bf16),
            vmem((n, CHIPS, RR, W), bf16),
            vmem((n, RR, W), bf16),
            vmem((n, RR, W), bf16),
            vmem((K, CHIPS, 2, ROWS, W), bf16),
            dma(5),
            dma(R),
            dma(R),
            dma(1),
            dma(1),
            dma(R),
            dma(R),
            dma(R),
            dma(R),
            dma(n),
            dma(n),
            dma(n),
            dma(n),
            dma(n),
            dma(n),
            dma(n),
            dma(n),
            dma(n, 2),
            dma(n, 2),
        ],
        compiler_params=pltpu.CompilerParams(
            collective_id=0, has_side_effects=True, vmem_limit_bytes=LIMIT * 2**20
        ),
        cost_estimate=pl.CostEstimate(flops=2 * 10**9, bytes_accessed=4 * 2**20, transcendentals=0),
        name="galore_step",
    )(*(pltpu.with_memory_space_constraint(v, pltpu.HBM) for v in (acts, grads_out, basis, first_moment, second_moment)))
    return update, *new_moments(first_moment, second_moment, proj)


IN_SPACE = pl.ANY
LIMIT = 24


def solution(mesh):
    return jax.shard_map(
        shards,
        mesh=mesh,
        in_specs=(
            P("dp", "fsdp"),
            P("dp", "fsdp"),
            P("fsdp", None),
            P("fsdp", "dp"),
            P("fsdp", "dp"),
        ),
        out_specs=(P("fsdp", "dp"), P("fsdp", "dp"), P("fsdp", "dp")),
        check_vma=False,
    )
```

```python
import jax
import jax.numpy as jnp
from jax import lax
from jax.experimental import pallas as pl
from jax.experimental.pallas import tpu as pltpu
from jax.sharding import PartitionSpec as P

bias_one = 1.0 - 0.9**10
bias_two = 1.0 - 0.999**10
adam_eps = 1e-08
galore_scale = 0.25

MESH = pl.DeviceIdType.MESH
bf16, f32 = jnp.bfloat16, jnp.float32

CHIPS = 8
ROWS = 32
TOK = 512
DEEP = 512
WIDE = 1536
HALF = WIDE // 2
R = 2
RR = ROWS // R
K = 2
W = WIDE // K
PARTS = [(r, k) for r in range(R) for k in range(K)]
STEPS = [
    ("reduce", 0),
    ("reduce", 1),
    ("moments", 0),
    ("reduce", 2),
    ("reduce", 3),
    ("moments", 1),
    ("moments", 2),
    ("moments", 3),
] + [(name, t) for t in range(len(PARTS)) for name in ("near", "far")]
FLUSH = {("reduce", 3), ("moments", 3), ("far", 3)}
FAR_FIRST = [(0, 0), (1, 2), (1, 1), (1, 3), (0, 2), (1, 0), (0, 1), (0, 3)]


def new_moments(first, second, proj):
    return 0.9 * first + 0.1 * proj, 0.999 * second + 0.001 * proj * proj


def kernel(
    acts_ref, g_ref, basis_ref, fm_ref, sm_ref,
    upd, proj_ref,
    acts, basis, g, fm, sm,
    pown, psend, precv, asend, arecv, pfull,
    q, qrecv, tsend, trecv, nfull,
    lsem, p_s, p_r, g_s, g_r, a_s, a_r, ag_s, ag_r, b_s, b_r, t_s, t_r,
    c_s, c_r, d_s, d_r, f_s, f_r,
):
    i, j = lax.axis_index("dp"), lax.axis_index("fsdp")
    m, c = j // 2, lax.rem(j, 2)
    other = 1 - c
    y, z_lo, z_hi, x = i // 2, lax.rem(i, 2), m // 4, lax.rem(m, 4)
    pair = (i, 2 * m + other)

    rows = [4 * lax.rem(z_hi + dz, 2) + lax.rem(x + dx, 4) for dz, dx in FAR_FIRST]
    cols_of = [2 * lax.rem(y + dy, 4) + lax.rem(z_lo + dz, 2) for dz, dy in FAR_FIRST]
    along = [4 * z_hi + lax.rem(x + d, 4) for d in range(4)]
    over = lax.rem(m + 4, CHIPS)
    row_peers = [(i, 2 * to + c) for to in rows]
    col_peers = [(to, j) for to in cols_of]

    def block_of(at):
        x_to = lax.rem(x + 6 + at // 2 - 2 * z_hi - x // 2, 4)
        return 4 * lax.rem(z_hi + at + x, 2) + x_to

    blocks = [block_of(to) for to in cols_of]
    row_to = blocks[0]
    z_from, x_from = i // 4, lax.rem(i, 4)
    y_from = lax.rem(x + 6 - x_from + 2 * z_from + x_from // 2, 4)
    i_from = 2 * y_from + lax.rem(z_hi + z_from + x_from, 2)
    stays = jnp.logical_and(m == i, row_to == m)
    turned, comes = (m, 2 * row_to + c), (i_from, 2 * i + c)

    def remote(src, dst, s, r, device):
        return pltpu.make_async_remote_copy(
            src_ref=src, dst_ref=dst, send_sem=s, recv_sem=r, device_id=device, device_id_type=MESH
        )

    sent = []

    def got(copy):
        copy.wait_recv()
        sent.append(copy)

    def got_all(ref, s, r):
        got(remote(ref, ref, s, r, pair))

    def flush():
        while sent:
            sent.pop(0).wait_send()

    g_here = g.at[:, pl.ds(pl.multiple_of(c * HALF, HALF), HALF)]
    loads = [
        pltpu.make_async_copy(acts_ref, acts, lsem.at[0]),
        pltpu.make_async_copy(basis_ref, basis, lsem.at[1]),
        pltpu.make_async_copy(g_ref, g_here, lsem.at[2]),
        pltpu.make_async_copy(fm_ref, fm, lsem.at[3]),
        pltpu.make_async_copy(sm_ref, sm, lsem.at[4]),
    ]
    for load in loads[:2]:
        load.start()

    barrier = pltpu.get_barrier_semaphore()
    for to in (*row_peers[1:], pair, *col_peers[1:]):
        pl.semaphore_signal(barrier, inc=1, device_id=to, device_id_type=MESH)

    @pl.when(jnp.logical_not(stays))
    def _():
        pl.semaphore_signal(barrier, inc=1, device_id=turned, device_id_type=MESH)
        pl.semaphore_signal(barrier, inc=1, device_id=comes, device_id_type=MESH)

    for load in loads[2:]:
        load.start()

    loads[0].wait()
    loads[1].wait()
    pown[...] = lax.dot_general(
        basis[...], acts[...], (((0,), (1,)), ((), ())), preferred_element_type=f32
    ).reshape(CHIPS, 2, ROWS, TOK)
    for r in range(R):
        psend[r] = pown[:, pl.ds(other, 1), r * RR : (r + 1) * RR].reshape(CHIPS, RR, TOK).astype(bf16)

    @pl.when(jnp.logical_not(stays))
    def _():
        pl.semaphore_wait(barrier, 2 * CHIPS + 1)

    @pl.when(stays)
    def _():
        pl.semaphore_wait(barrier, 2 * CHIPS - 1)

    to_pair = [remote(psend.at[r], precv.at[r], p_s.at[r], p_r.at[r], pair) for r in range(R)]
    for copy in to_pair:
        copy.start()
    loads[2].wait()
    g_pair = remote(g_here, g_here, g_s.at[0], g_r.at[0], pair)
    g_pair.start()

    a_copies = [
        [
            remote(
                asend.at[r, rows[d]],
                arecv.at[r, d],
                a_s.at[r],
                a_r.at[r],
                row_peers[d],
            )
            for d in range(1, CHIPS)
        ]
        for r in range(R)
    ]
    for r in range(R):
        got(to_pair[r])
        asend[r] = (
            pown[:, pl.ds(c, 1), r * RR : (r + 1) * RR].reshape(CHIPS, RR, TOK)
            + precv[r].astype(f32)
        ).astype(bf16)
        for copy in a_copies[r]:
            copy.start()
    ag_copies = [
        [
            remote(
                pfull.at[r, m],
                pfull.at[r, m],
                ag_s.at[r],
                ag_r.at[r],
                row_peers[d],
            )
            for d in range(1, CHIPS)
        ]
        for r in range(R)
    ]
    for r in range(R):
        total = asend[r, m].astype(f32)
        got_all(arecv.at[r, pl.ds(1, CHIPS - 1)], a_s.at[r], a_r.at[r])
        for d in range(1, CHIPS):
            total += arecv[r, d].astype(f32)
        pfull[r, m] = total.astype(bf16)
        for copy in ag_copies[r]:
            copy.start()

    b_copies = []
    for t, (r, k) in enumerate(PARTS):
        if k == 0:
            got_all(arecv.at[r, pl.ds(1, CHIPS - 1)], ag_s.at[r], ag_r.at[r])
        if t == 0:
            got(g_pair)
        q[t] = (
            jnp.dot(
                pfull[r].reshape(CHIPS * RR, TOK),
                g[:, k * W : (k + 1) * W],
                preferred_element_type=f32,
            )
            .astype(bf16)
            .reshape(CHIPS, RR, W)
        )
        b_copies.append(
            [
                remote(
                    q.at[t, blocks[d]],
                    qrecv.at[t, d],
                    b_s.at[t],
                    b_r.at[t],
                    col_peers[d],
                )
                for d in range(1, CHIPS)
            ]
        )
        for copy in b_copies[t]:
            copy.start()
    loads[3].wait()
    loads[4].wait()
    flush()

    def turn(t):
        return remote(tsend.at[t], trecv.at[t], t_s.at[t], t_r.at[t], turned)

    def reduce(t):
        total = q[t, row_to].astype(f32)
        got_all(qrecv.at[t, pl.ds(1, CHIPS - 1)], b_s.at[t], b_r.at[t])
        for d in range(1, CHIPS):
            total += qrecv[t, d].astype(f32)
        tsend[t] = total.astype(bf16)

        @pl.when(jnp.logical_not(stays))
        def _():
            turn(t).start()

        @pl.when(stays)
        def _():
            trecv[t] = total.astype(bf16)

    near_copies, far_copies, shares = {}, {}, {}
    lines = [slice(r * RR, (r + 1) * RR) for r in range(R)]

    def along_x(t):
        block = nfull.at[PARTS[t][1], m, c, lines[PARTS[t][0]]]
        copies = []
        for d in (2, 1, 3):
            copies.append(remote(block, block, c_s.at[t], c_r.at[t], (i, 2 * along[d] + c)))
            copies[-1].start()
        return copies

    def beyond(t):
        block = nfull.at[PARTS[t][1], m, c, lines[PARTS[t][0]]]
        copies = []
        for d in (2, 1, 3):
            to = lax.rem(along[d] + 4, CHIPS)
            copies.append(remote(block, block, d_s.at[t], d_r.at[t], (i, 2 * to + c)))
            copies[-1].start()
        return copies

    def across(t):
        mine = nfull.at[PARTS[t][1], m, c, lines[PARTS[t][0]]]
        return remote(mine, mine, d_s.at[t], d_r.at[t], (i, 2 * over + c))

    def to_other_core(t, first, n):
        part = nfull.at[PARTS[t][1], pl.ds(first, 4), c, lines[PARTS[t][0]]]
        shares[t, n] = remote(part, part, f_s.at[t, n], f_r.at[t, n], pair)
        shares[t, n].start()

    def moments(t):
        @pl.when(jnp.logical_not(stays))
        def _():
            turn(t).wait_recv()

        r, k = PARTS[t]
        cols = slice(k * W, (k + 1) * W)
        proj = trecv[t].astype(f32)
        one, two = new_moments(fm[lines[r], cols], sm[lines[r], cols], proj)
        nfull[k, m, c, lines[r]] = (
            one / bias_one / (jnp.sqrt(two / bias_two) + adam_eps)
        ).astype(bf16)
        far_copies[t] = beyond(t)
        across(t).start()
        near_copies[t] = along_x(t)
        proj_ref[lines[r], cols] = proj

    def near(t):
        got_all(nfull.at[PARTS[t][1], pl.ds(0, 3), c, lines[PARTS[t][0]]], c_s.at[t], c_r.at[t])
        to_other_core(t, 4 * z_hi, 0)

    def far(t):
        got_all(nfull.at[PARTS[t][1], pl.ds(0, 4), c, lines[PARTS[t][0]]], d_s.at[t], d_r.at[t])
        to_other_core(t, 4 * (1 - z_hi), 1)

    def update(k):
        for t in range(len(PARTS)):
            if PARTS[t][1] == k:
                got(shares[t, 0])
                got(shares[t, 1])
        cols = slice(k * W, (k + 1) * W)
        upd[:, cols] = (
            galore_scale
            * jnp.dot(
                basis[...], nfull[k].reshape(CHIPS * 2 * ROWS, W), preferred_element_type=f32
            )
        ).astype(bf16)

    steps = {"reduce": reduce, "moments": moments, "near": near, "far": far}
    pending = []
    for name, t in STEPS:
        steps[name](t)
        if (name, t) in FLUSH:
            flush()
        if pending and name in ("near", "far"):
            update(pending.pop())
        if name == "far" and PARTS[t][0] == R - 1:
            pending.append(PARTS[t][1])
    for k in pending:
        update(k)
    flush()

    @pl.when(jnp.logical_not(stays))
    def _():
        for t in range(len(PARTS)):
            turn(t).wait_send()


def shards(acts, grads_out, basis, first_moment, second_moment):
    def vmem(shape, dtype):
        return pltpu.VMEM(shape, dtype)

    def dma(*shape):
        return pltpu.SemaphoreType.DMA(shape)

    n = len(PARTS)
    update, proj = pl.pallas_call(
        kernel,
        out_shape=(
            jax.ShapeDtypeStruct((DEEP, WIDE), bf16),
            jax.ShapeDtypeStruct((ROWS, WIDE), f32),
        ),
        in_specs=[pl.BlockSpec(memory_space=IN_SPACE)] * 5,
        out_specs=(pl.BlockSpec(memory_space=pltpu.VMEM),) * 2,
        scratch_shapes=[
            vmem((TOK, DEEP), bf16),
            vmem((DEEP, 512), bf16),
            vmem((TOK, WIDE), bf16),
            vmem((ROWS, WIDE), f32),
            vmem((ROWS, WIDE), f32),
            vmem((CHIPS, 2, ROWS, TOK), f32),
            vmem((R, CHIPS, RR, TOK), bf16),
            vmem((R, CHIPS, RR, TOK), bf16),
            vmem((R, CHIPS, RR, TOK), bf16),
            vmem((R, CHIPS, RR, TOK), bf16),
            vmem((R, CHIPS, RR, TOK), bf16),
            vmem((n, CHIPS, RR, W), bf16),
            vmem((n, CHIPS, RR, W), bf16),
            vmem((n, RR, W), bf16),
            vmem((n, RR, W), bf16),
            vmem((K, CHIPS, 2, ROWS, W), bf16),
            dma(5),
            dma(R),
            dma(R),
            dma(1),
            dma(1),
            dma(R),
            dma(R),
            dma(R),
            dma(R),
            dma(n),
            dma(n),
            dma(n),
            dma(n),
            dma(n),
            dma(n),
            dma(n),
            dma(n),
            dma(n, 2),
            dma(n, 2),
        ],
        compiler_params=pltpu.CompilerParams(
            collective_id=0, has_side_effects=True, vmem_limit_bytes=LIMIT * 2**20
        ),
        cost_estimate=pl.CostEstimate(flops=2 * 10**9, bytes_accessed=4 * 2**20, transcendentals=0),
        name="galore_step",
    )(*(pltpu.with_memory_space_constraint(v, pltpu.HBM) for v in (acts, grads_out, basis, first_moment, second_moment)))
    return update, *new_moments(first_moment, second_moment, proj)


IN_SPACE = pl.ANY
LIMIT = 24


def solution(mesh):
    return jax.shard_map(
        shards,
        mesh=mesh,
        in_specs=(
            P("dp", "fsdp"),
            P("dp", "fsdp"),
            P("fsdp", None),
            P("fsdp", "dp"),
            P("fsdp", "dp"),
        ),
        out_specs=(P("fsdp", "dp"), P("fsdp", "dp"), P("fsdp", "dp")),
        check_vma=False,
    )
```
